512 devices in a mesh: pair: 128 (over x, y_lo, z), view: 2 (over y_hi), head: 2 (over core).
Axes of the slice: x: 4, y: 4 (y_hi: 2, y_lo: 2; y = y_hi * 2 + y_lo), z: 16, core: 2. Of those that a mesh axis runs over, the one named last changes fastest.
Arguments:
- enc_tokens: bfloat16 [128, 512, 1024], P('pair', ('view', 'head')), may hold values from -6 to 6
- pairs: int32 [128, 2], replicated, may hold values from 0 to 127, all different within a row
- image_slot: int32 [128], replicated, may hold values from 0 to 127, each once
- embed_weight: bfloat16 [1024, 768], replicated, may hold values from -0.1875 to 0.1875
- norm_gains: float32 [2, 2, 768], P('view'), may hold values from 0.5 to 1.5
- cross_q: bfloat16 [2, 768, 768], P('view', None, 'head'), may hold values from -1 to 1
- cross_kv: bfloat16 [2, 768, 2, 768], P('view', None, None, 'head'), may hold values from -4 to 4
- cross_out: bfloat16 [2, 768, 768], P('view', None, 'head'), may hold values from -0.21875 to 0.21875
Outputs:
- joined: bfloat16 [128, 512, 768], P('pair', ('view', 'head'))
The draws below stay inside these ranges and needn't reach their ends.
Inputs may be any that keep to these rules, and one draw needn't show every extreme that they name: `pairs`: each row names two different images, and every image is named by some row. `image_slot`: each image has its own slot.
All inputs are finite; a program needn't handle non-finite values.
Results may differ from the reference program's by a relative error of at most 0.0064.
Values may be sent and summed in bfloat16 or wider, within the bound.
A program may use at most 64 MiB of HBM per device.

```python
import jax
import jax.numpy as jnp
from jax import lax

ENC = 1024
DD = 768
HEADS = 12
HD = 64
GRIDW = 32
VIEWS = 2
TOK = 512
IMAGES = 128
PAIRS = 128


def shared_base(key):
    return jax.random.normal(key, (VIEWS, DD, HEADS * HD), jnp.float32)


def draw_enc_tokens(key, part):
    key = jax.random.fold_in(key, 13)
    key_own = jax.random.fold_in(key, 0)
    own_part = jax.random.normal(key_own, (IMAGES, TOK, ENC), jnp.float32)
    result = own_part
    return jnp.clip(result, -6.0, 6.0).astype(jnp.bfloat16)


def draw_cross_q(key, part):
    base_matrix = shared_base(key)
    result = base_matrix * DD ** (-0.5)
    return jnp.clip(result, -1.0, 1.0).astype(jnp.bfloat16)


def draw_cross_kv(key, part):
    key = jax.random.fold_in(key, 12)
    key_fresh = jax.random.fold_in(key, 0)
    fresh = jax.random.normal(key_fresh, (VIEWS, DD, 2, HEADS * HD), jnp.float32) * DD ** (-0.5)
    result = fresh
    return jnp.clip(result, -4.0, 4.0).astype(jnp.bfloat16)


def steps_of(rng, extent, pieces, smallest, high):
    def one(dim, parts):
        heights = jax.random.uniform(jax.random.fold_in(jax.random.fold_in(rng, 6), dim), (parts,), jnp.float32, smallest / len(pieces), high / len(pieces))
        return jnp.repeat(jnp.exp(heights), extent[dim] // parts).reshape((-1,) + (1,) * (len(extent) - dim - 1))

    loudness = one(*pieces[0])
    for cut in pieces[1:]:
        loudness = loudness * one(*cut)
    return loudness


def choose_distinct(key, rows, amount, top, lift):
    sequence = jax.random.permutation(jax.random.fold_in(key, 1), amount)
    favour = sequence
    for power in range(3):
        favour = favour * favour // amount
    favour = favour * lift // amount
    tickets = jax.random.randint(jax.random.fold_in(key, 2), (rows, amount), 0, 4096) + favour
    holders = jax.random.permutation(jax.random.fold_in(key, 3), rows)[jnp.arange(amount) % rows]
    tickets = jnp.where(jnp.arange(rows)[:, None] == holders[None, :], 1 << 14, tickets)
    score = tickets * amount + jnp.arange(amount)
    return lax.top_k(score.astype(jnp.int32), top)[1].astype(jnp.int32)


def noise(own_key, dims, deviation, limit, cuts=(), kind=jnp.bfloat16):
    level = steps_of(own_key, dims, cuts, -0.22, 0.18) if cuts else 1.0
    values = jax.random.normal(own_key, dims, jnp.float32) * deviation * level
    return jnp.minimum(jnp.maximum(values, -limit), limit).astype(kind)


def setup_inputs(seed: int = 0) -> dict:
    keys = jax.random.split(jax.random.key(seed), 9)
    enc_tokens = draw_enc_tokens(jax.random.fold_in(keys[8], 71), 0)
    pairs = choose_distinct(keys[1], PAIRS, IMAGES, 2, 256)
    image_slot = jax.random.permutation(keys[2], IMAGES).astype(jnp.int32)
    embed_weight = noise(keys[3], (ENC, DD), ENC ** -0.5, 0.1875)
    norm_gains = jnp.clip(1.0 + 0.1 * jax.random.normal(keys[4], (VIEWS, 2, DD), jnp.float32), 0.5, 1.5)
    cross_q = draw_cross_q(jax.random.fold_in(keys[8], 71), 0)
    cross_kv = draw_cross_kv(jax.random.fold_in(keys[8], 71), 0)
    cross_out = noise(keys[7], (VIEWS, DD, HEADS * HD), (HEADS * HD) ** -0.5, 0.21875, ((0, 2), (2, 2)))
    return dict(enc_tokens=enc_tokens, pairs=pairs, image_slot=image_slot, embed_weight=embed_weight, norm_gains=norm_gains, cross_q=cross_q, cross_kv=cross_kv, cross_out=cross_out)


def normalize(inputs, gain):
    inputs = inputs.astype(jnp.float32)
    centered = inputs - lax.optimization_barrier(jnp.mean(inputs, axis=-1, keepdims=True))
    variance = lax.optimization_barrier(jnp.mean(centered * centered, axis=-1, keepdims=True))
    return (centered * lax.rsqrt(variance + 1e-06) * gain).astype(jnp.bfloat16)

def rotate(inputs, head_dim, grid_width):
    token_count = inputs.shape[0]
    half_dim = head_dim // 2
    quarter_dim = half_dim // 2
    split_up = inputs.reshape(token_count, -1, 2, 2, quarter_dim)
    row_index = jnp.arange(token_count, dtype=jnp.int32)
    places = jnp.stack([row_index // grid_width, row_index % grid_width], axis=1).astype(jnp.float32)
    frequency = 100.0 ** (-2.0 * jnp.arange(quarter_dim, dtype=jnp.float32) / half_dim)
    angles = places[:, None, :, None] * frequency
    cosine = jnp.cos(angles)
    sine_table = jnp.sin(angles)
    first_part = split_up[:, :, :, 0, :]
    second_part = split_up[:, :, :, 1, :]
    turned = jnp.stack([first_part * cosine - second_part * sine_table, second_part * cosine + first_part * sine_table], axis=3)
    return turned.reshape(inputs.shape)

def attend(queries, key_rows, value_rows, head_dim):
    token_count = queries.shape[0]
    query_heads = queries.reshape(token_count, -1, head_dim).astype(jnp.float32)
    key_heads = key_rows.reshape(key_rows.shape[0], -1, head_dim).astype(jnp.float32)
    value_heads = value_rows.reshape(value_rows.shape[0], -1, head_dim).astype(jnp.float32)
    scores = jnp.einsum('qhd,khd->hqk', query_heads, key_heads) * head_dim ** (-0.5)
    row_top = lax.optimization_barrier(jnp.max(scores, axis=-1, keepdims=True))
    expo = jnp.exp(scores - row_top)
    row_total = lax.optimization_barrier(jnp.sum(expo, axis=-1, keepdims=True))
    weights = (expo / row_total).astype(jnp.bfloat16)
    attended = jnp.einsum('hqk,khd->qhd', weights.astype(jnp.float32), value_heads)
    return attended.astype(jnp.bfloat16).reshape(token_count, -1)

def branch(own_tokens, partner, branch_gains, query_weight, pair_weight, out_weight):
    query_in = normalize(own_tokens, branch_gains[0])
    key_in = normalize(partner, branch_gains[1])
    queries = rotate(jnp.dot(query_in, query_weight, preferred_element_type=jnp.float32), HD, GRIDW).astype(jnp.bfloat16)
    projected = jnp.einsum('td,dch->tch', key_in.astype(jnp.float32), pair_weight.astype(jnp.float32))
    key_rows = rotate(projected[:, 0], HD, GRIDW).astype(jnp.bfloat16)
    value_rows = projected[:, 1].astype(jnp.bfloat16)
    attended = attend(queries, key_rows, value_rows, HD)
    crossed = lax.dot_general(attended, out_weight, (((1,), (1,)), ((), ())), preferred_element_type=jnp.float32)
    return own_tokens.astype(jnp.float32) + crossed

def reference(enc_tokens, pairs, image_slot, embed_weight, norm_gains, cross_q, cross_kv, cross_out):
    flattened = enc_tokens.reshape(IMAGES * TOK, ENC)
    embedded = jnp.dot(flattened, embed_weight, preferred_element_type=jnp.float32).astype(jnp.bfloat16).reshape(IMAGES, TOK, DD)
    by_image = embedded[image_slot]
    use_count = lax.optimization_barrier(jnp.sum((pairs.reshape(-1)[None, :] == jnp.arange(IMAGES, dtype=jnp.int32)[:, None]).astype(jnp.int32), axis=1))

    def add_pair(totals, pair_entry):
        first_image = pair_entry[0]
        second_image = pair_entry[1]
        first_tokens = by_image[first_image]
        second_tokens = by_image[second_image]
        first_update = branch(first_tokens, second_tokens, norm_gains[0], cross_q[0], cross_kv[0], cross_out[0])
        second_update = branch(second_tokens, first_tokens, norm_gains[1], cross_q[1], cross_kv[1], cross_out[1])
        totals = totals.at[first_image].add(first_update)
        totals = totals.at[second_image].add(second_update)
        return (totals, None)
    totals, _ = lax.scan(add_pair, jnp.zeros((IMAGES, TOK, DD), jnp.float32), pairs)
    average = totals / use_count.astype(jnp.float32)[:, None, None]
    return jnp.zeros((IMAGES, TOK, DD), jnp.bfloat16).at[image_slot].set(average.astype(jnp.bfloat16))
```

```python
import jax
import jax.numpy as jnp
import numpy as np
from jax import lax
from jax.experimental import pallas as pl
from jax.experimental.pallas import tpu as pltpu
from jax.sharding import PartitionSpec as P

HD = 64
GRIDW = 32
TOK = 512
DD = 768
HALF = 384
NP = 128
BF = jnp.bfloat16
F32 = jnp.float32
MESH = pl.DeviceIdType.MESH


def rope_tables():
    lane = np.arange(128)
    token = np.arange(TOK)
    place = np.where(
        ((lane % HD) // 32)[None, :] == 0, (token // GRIDW)[:, None], (token % GRIDW)[:, None]
    ).astype(np.float64)
    frequency = 100.0 ** (-2.0 * (lane % 16) / 32.0)
    angle = place * frequency[None, :]
    sign = np.where((lane % 32) < 16, -1.0, 1.0)
    return np.cos(angle).astype(np.float32), (np.sin(angle) * sign[None, :]).astype(np.float32)


def iota(shape, dim):
    return lax.broadcasted_iota(jnp.int32, shape, dim)


def onehot(mask):
    return jnp.where(mask, 1.0, 0.0).astype(BF)


def dot(a, b, dims=((1,), (0,))):
    return lax.dot_general(a, b, (dims, ((), ())), preferred_element_type=F32)


def kernel(
    x_ref, pairs_ref, slot_ref, emb_ref, gain_ref, wq_ref, wkv_ref, wo_ref, cos_ref, sin_ref,
    out_ref,
    e_ref, s1, h_ref, s2, t_ref, f_ref, wk, wv, wox, qkv, att, attx, yb, yx, s3, r_ref, s4, z_ref,
    local_sem, wo_sem, p1, p2, ysem, csem, fsem, asem, bsem, p3, p4,
):
    me = lax.axis_index("pair")
    view = lax.axis_index("view")
    core = lax.axis_index("head")
    mine = view * 2 + core
    across = view * 2 + 1 - core
    to_core = {"head": 1 - core}
    to_view = {"view": 1 - view}

    def remote(src, dst, sems, where):
        return pltpu.make_async_remote_copy(
            src, dst, sems.at[0], sems.at[1], device_id=where, device_id_type=MESH
        )

    barrier = pltpu.get_barrier_semaphore()

    def greet(k, carry):
        pl.semaphore_signal(
            barrier, inc=1, device_id={"pair": lax.rem(me + k, NP)}, device_id_type=MESH
        )
        return carry

    pl.semaphore_signal(barrier, inc=1, device_id=to_core, device_id_type=MESH)
    pl.semaphore_signal(barrier, inc=1, device_id=to_view, device_id_type=MESH)
    lax.fori_loop(1, NP, greet, 0)

    def scatter(src, dst, sems):
        def send(k, carry):
            peer = lax.rem(me + k, NP)
            remote(src.at[peer], dst.at[me], sems, {"pair": peer}).start()
            return carry

        lax.fori_loop(1, NP, send, 0)

    def landed(buf, sem):
        whole = buf.at[pl.ds(0, NP - 1)]
        pltpu.make_async_copy(whole, whole, sem).wait()

    weave = [onehot(iota((2 * NP, NP), 0) == 2 * iota((2 * NP, NP), 1) + f) for f in range(2)]
    part = [onehot(iota((NP, 2 * NP), 1) == 2 * iota((NP, 2 * NP), 0) + f) for f in range(2)]

    def interleave(rows):
        mixed = dot(weave[0], rows[:, :HALF]) + dot(weave[1], rows[:, HALF:])
        return mixed.astype(BF).reshape(NP, 2, HALF)

    def separate(rows):
        flat = rows.reshape(2 * NP, HALF)
        return dot(part[0], flat), dot(part[1], flat)

    e_ref[...] = dot(x_ref[...], emb_ref[...]).astype(BF)
    s1[...] = interleave(e_ref[...])
    pl.semaphore_wait(barrier, NP + 1)
    scatter(s1, h_ref, p1)
    h_ref[me] = s1[me]
    remote(wo_ref, wox, wo_sem, to_core).start()

    pair_col = dot(
        onehot(iota((2 * NP, NP), 0) // 2 == iota((2 * NP, NP), 1)), pairs_ref[...].astype(BF)
    )
    slot_rows = onehot(iota((2 * NP, NP), 0) // 2 == slot_ref[...])
    same = (iota((2 * NP, 2 * NP), 0) - iota((2 * NP, 2 * NP), 1)) % 2 == 0
    pick, spread = [], []
    for b in range(2):
        image = onehot(iota((2 * NP, NP), 1) == pair_col[:, b : b + 1].astype(jnp.int32))
        pick.append(jnp.where(same, dot(image, slot_rows, ((1,), (1,))), 0.0).astype(BF))
        spread.append(jnp.where(same, dot(slot_rows, image, ((1,), (1,))), 0.0).astype(BF))
    uses = jnp.sum(spread[0].astype(F32) + spread[1].astype(F32), axis=1, keepdims=True)

    for block in range(DD // NP):
        first, second = separate(wkv_ref[block * NP : (block + 1) * NP])
        wk[block * NP : (block + 1) * NP, :] = first.astype(BF)
        wv[block * NP : (block + 1) * NP, :] = second.astype(BF)

    landed(h_ref, p1.at[1])
    held = h_ref[...].reshape(2 * NP, HALF)
    for b in range(2):
        s2[b] = dot(pick[b], held).astype(BF).reshape(NP, 2, HALF)
        scatter(s2.at[b], t_ref.at[b], p2.at[b])
        t_ref[b, me] = s2[b, me]

    for b in range(2):
        landed(t_ref.at[b], p2.at[b, 1])
        first, second = separate(t_ref[b])
        f_ref[b, mine, :, :HALF] = first.astype(BF)
        f_ref[b, mine, :, HALF:] = second.astype(BF)
        remote(f_ref.at[b, mine], f_ref.at[b, mine], ysem.at[b], to_view).start()
        remote(f_ref.at[b, mine], f_ref.at[b, mine], csem.at[b], to_core).start()
    there = (1 - view) * 2 + core
    for b in range(2):
        arrived = f_ref.at[b, there]
        pltpu.make_async_copy(arrived, arrived, ysem.at[b, 1]).wait()
        remote(arrived, arrived, fsem.at[b], to_core).start()
    for b in range(2):
        block = f_ref.at[b, mine]
        pltpu.make_async_copy(block, block, csem.at[b, 1]).wait()
        pltpu.make_async_copy(block, block, fsem.at[b, 1]).wait()

    def normalize(rows, gain):
        rows = rows.astype(F32)
        centered = rows - jnp.mean(rows, axis=-1, keepdims=True)
        variance = jnp.mean(centered * centered, axis=-1, keepdims=True)
        return (centered * lax.rsqrt(variance + 1e-06) * gain).astype(BF)

    low16 = iota((NP, 128), 1) % 32 < 16

    def rotate(rows, cosine, sine, scale):
        parts = []
        for block in range(HALF // 128):
            u = rows[:, block * 128 : (block + 1) * 128]
            swapped = jnp.where(low16, pltpu.roll(u, 112, 1), pltpu.roll(u, 16, 1))
            parts.append((u * cosine + swapped * sine).astype(BF) * scale)
        return jnp.concatenate(parts, axis=1)

    def project(quarter, carry):
        rows = pl.ds(pl.multiple_of(quarter * NP, NP), NP)
        cosine, sine = cos_ref[rows, :], sin_ref[rows, :]
        query_in = normalize(f_ref[view, quarter], gain_ref[0:1, :])
        qkv[0, rows, :] = rotate(dot(query_in, wq_ref[...]), cosine, sine, BF(HD**-0.5))
        key_in = normalize(f_ref[1 - view, quarter], gain_ref[1:2, :])
        qkv[1, rows, :] = rotate(dot(key_in, wk[...]), cosine, sine, BF(1.0))
        qkv[2, rows, :] = dot(key_in, wv[...]).astype(BF)
        return carry

    lax.fori_loop(0, 4, project, 0)

    wox_wait = remote(wo_ref, wox, wo_sem, to_core)
    wox_wait.wait_recv()

    left_q = iota((2 * NP, 128), 1) < HD
    left_k = iota((TOK, 128), 1) < HD
    one = jnp.ones((), BF)
    zero = jnp.zeros((), BF)
    for step in range(2):
        half = 1 - view if step == 0 else view
        rows = pl.ds(pl.multiple_of(half * 2 * NP, 2 * NP), 2 * NP)
        for block in range(HALF // 128):
            columns = slice(block * 128, (block + 1) * 128)
            queries = qkv[0, rows, columns]
            keys = qkv[1, :, columns]
            values = qkv[2, :, columns]
            results = []
            for side in range(2):
                own_q = left_q if side == 0 else jnp.logical_not(left_q)
                own_k = left_k if side == 0 else jnp.logical_not(left_k)
                scores = dot(jnp.where(own_q, queries, zero), keys, ((1,), (1,)))
                expo = jnp.exp(scores - jnp.max(scores, axis=-1, keepdims=True)).astype(BF)
                results.append(dot(expo, jnp.where(own_k, values, one)))
            top = jnp.where(left_q, results[0], results[1])
            total = pltpu.roll(jnp.where(left_q, results[1], results[0]), HD, 1)
            attended = (top / total).astype(BF)
            att[step, 0, :, columns] = attended[:NP]
            att[step, 1, :, columns] = attended[NP:]
        remote(att.at[step, 1 - core], attx.at[step], asem.at[step], to_core).start()
        pltpu.make_async_copy(attx.at[step], attx.at[step], asem.at[step, 1]).wait()
        crossed = dot(att[step, core], wo_ref[...], ((1,), (1,)))
        crossed = (crossed + dot(attx[step], wox[...], ((1,), (1,)))).astype(BF)
        if step == 0:
            yb[...] = interleave(crossed)
            remote(yb, yx, bsem, to_view).start()
        else:
            s3[:, view] = interleave(crossed)
    pltpu.make_async_copy(yx, yx, bsem.at[1]).wait()
    s3[:, 1 - view] = yx[...]

    scatter(s3, r_ref, p3)
    r_ref[me] = s3[me]
    landed(r_ref, p3.at[1])
    total = dot(spread[0], r_ref[:, 0].reshape(2 * NP, HALF))
    total = total + dot(spread[1], r_ref[:, 1].reshape(2 * NP, HALF))
    s4[...] = (total / uses).astype(BF).reshape(NP, 2, HALF)
    scatter(s4, z_ref, p4)
    z_ref[me] = s4[me]
    landed(z_ref, p4.at[1])
    first, second = separate(z_ref[...])
    out_ref[:, :HALF] = (e_ref[:, :HALF].astype(F32) + first).astype(BF)
    out_ref[:, HALF:] = (e_ref[:, HALF:].astype(F32) + second).astype(BF)

    landed(s1, p1.at[0])
    for b in range(2):
        landed(s2.at[b], p2.at[b, 0])
        block = f_ref.at[b, mine]
        pltpu.make_async_copy(block, block, ysem.at[b, 0]).wait()
        pltpu.make_async_copy(block, block, csem.at[b, 0]).wait()
        pltpu.make_async_copy(block, block, fsem.at[b, 0]).wait()
        pltpu.make_async_copy(attx.at[b], attx.at[b], asem.at[b, 0]).wait()
    wox_wait.wait_send()
    pltpu.make_async_copy(yb, yb, bsem.at[0]).wait()
    landed(s3, p3.at[0])
    landed(s4, p4.at[0])


def body(enc_tokens, pairs, image_slot, embed_weight, norm_gains, cross_q, cross_kv, cross_out):
    cosine, sine = rope_tables()
    vmem = pl.BlockSpec(memory_space=pltpu.VMEM)
    message = (NP, 2, HALF)
    sems = pltpu.SemaphoreType.DMA
    out = pl.pallas_call(
        kernel,
        out_shape=jax.ShapeDtypeStruct((NP, DD), BF),
        in_specs=[vmem] * 10,
        out_specs=vmem,
        scratch_shapes=[
            pltpu.VMEM((NP, DD), BF),
            pltpu.VMEM(message, BF),
            pltpu.VMEM(message, BF),
            pltpu.VMEM((2,) + message, BF),
            pltpu.VMEM((2,) + message, BF),
            pltpu.VMEM((2, 4, NP, DD), BF),
            pltpu.VMEM((DD, HALF), BF),
            pltpu.VMEM((DD, HALF), BF),
            pltpu.VMEM((DD, HALF), BF),
            pltpu.VMEM((3, TOK, HALF), BF),
            pltpu.VMEM((2, 2, NP, HALF), BF),
            pltpu.VMEM((2, NP, HALF), BF),
            pltpu.VMEM(message, BF),
            pltpu.VMEM(message, BF),
            pltpu.VMEM((NP, 2, 2, HALF), BF),
            pltpu.VMEM((NP, 2, 2, HALF), BF),
            pltpu.VMEM(message, BF),
            pltpu.VMEM(message, BF),
            sems,
            sems((2,)),
            sems((2,)),
            sems((2, 2)),
            sems((2, 2)),
            sems((2, 2)),
            sems((2, 2)),
            sems((2, 2)),
            sems((2,)),
            sems((2,)),
            sems((2,)),
        ],
        compiler_params=pltpu.CompilerParams(
            collective_id=0, has_side_effects=True, vmem_limit_bytes=56 << 20
        ),
        name="cross_block",
    )(
        enc_tokens[0],
        pairs,
        image_slot.reshape(1, NP),
        embed_weight,
        norm_gains[0],
        cross_q[0],
        cross_kv[0],
        cross_out[0],
        cosine,
        sine,
    )
    return out[None]


def solution(mesh):
    placed = (
        P("pair", ("view", "head"), None),
        P(),
        P(),
        P(),
        P("view", None, None),
        P("view", None, "head"),
        P("view", None, None, "head"),
        P("view", None, "head"),
    )
    return jax.shard_map(
        body,
        mesh=mesh,
        in_specs=placed,
        out_specs=P("pair", ("view", "head"), None),
        check_vma=False,
    )
```

```python
import jax
import jax.numpy as jnp
import numpy as np
from jax import lax
from jax.experimental import pallas as pl
from jax.experimental.pallas import tpu as pltpu
from jax.sharding import PartitionSpec as P

HD = 64
GRIDW = 32
TOK = 512
DD = 768
HALF = 384
NP = 128
BF = jnp.bfloat16
F32 = jnp.float32
MESH = pl.DeviceIdType.MESH
THROTTLE1 = False
THROTTLE2 = True
THROTTLE3 = True


def rope_tables():
    lane = np.arange(128)
    token = np.arange(TOK)
    place = np.where(
        ((lane % HD) // 32)[None, :] == 0, (token // GRIDW)[:, None], (token % GRIDW)[:, None]
    ).astype(np.float64)
    frequency = 100.0 ** (-2.0 * (lane % 16) / 32.0)
    angle = place * frequency[None, :]
    sign = np.where((lane % 32) < 16, -1.0, 1.0)
    return np.cos(angle).astype(np.float32), (np.sin(angle) * sign[None, :]).astype(np.float32)


def iota(shape, dim):
    return lax.broadcasted_iota(jnp.int32, shape, dim)


def onehot(mask):
    return jnp.where(mask, 1.0, 0.0).astype(BF)


def dot(a, b, dims=((1,), (0,))):
    return lax.dot_general(a, b, (dims, ((), ())), preferred_element_type=F32)


def kernel(
    x_hbm, pairs_ref, slot_ref, emb_hbm, gain_ref, wq_hbm, wkv_hbm, wo_hbm, cos_hbm, sin_hbm,
    e_ref, avg_ref,
    x_ref, emb_ref, wq_ref, wkv_ref, wo_ref, cos_ref, sin_ref,
    s1, h_ref, s2, t_ref, f_ref, wk, wv, wox, qkv, att, attx, s3, r_ref, s4, z_ref,
    in_sem, wo_sem, p1, p2, ysem, csem, fsem, asem, p3, p4,
):
    me = lax.axis_index("pair")
    view = lax.axis_index("view")
    core = lax.axis_index("head")
    mine = view * 2 + core
    half_me = me // 2
    odd_me = me - 2 * half_me
    to_core = {"head": 1 - core}
    to_view = {"view": 1 - view}

    def remote(src, dst, sent, got, where):
        return pltpu.make_async_remote_copy(
            src, dst, sent, got, device_id=where, device_id_type=MESH
        )

    def arrive(buf, sem):
        pltpu.make_async_copy(buf, buf, sem).wait()

    def landed(buf, sem, count=NP - 1):
        arrive(buf.at[pl.ds(0, count)], sem)

    loads = [
        pltpu.make_async_copy(src, dst, in_sem.at[i])
        for i, (src, dst) in enumerate(
            (
                (x_hbm, x_ref),
                (emb_hbm, emb_ref),
                (wo_hbm, wo_ref),
                (wkv_hbm, wkv_ref),
                (wq_hbm, wq_ref),
                (cos_hbm, cos_ref),
                (sin_hbm, sin_ref),
            )
        )
    ]
    for load in loads:
        load.start()

    barrier = pltpu.get_barrier_semaphore()

    def greet(k, carry):
        pl.semaphore_signal(
            barrier, inc=1, device_id={"pair": lax.rem(me + k, NP)}, device_id_type=MESH
        )
        return carry

    lax.fori_loop(1, NP, greet, 0)
    pl.semaphore_signal(barrier, inc=1, device_id=to_core, device_id_type=MESH)
    pl.semaphore_signal(barrier, inc=1, device_id=to_view, device_id_type=MESH)

    def scatter(src, dst, sent, got, first=1, last=NP):
        def send(k, carry):
            peer = lax.rem(me + k, NP)
            remote(src.at[peer], dst, sent, got, {"pair": peer}).start()
            return carry

        lax.fori_loop(first, last, send, 0)

    def scatter_half(src, dst, sent, got, parity, where=None):
        def send(i, carry):
            peer = 2 * lax.rem(half_me + i, NP // 2) + parity
            target = {"pair": peer} if where is None else {"pair": peer, **where}
            copy = remote(src.at[peer], dst, sent, got, target)
            if where is None:
                pl.when(peer != me)(copy.start)
            else:
                copy.start()
            return carry

        lax.fori_loop(0, NP // 2, send, 0)

    def half_left(buf, sem, parity):
        @pl.when(odd_me == parity)
        def _():
            landed(buf, sem, NP // 2 - 1)

        @pl.when(odd_me != parity)
        def _():
            landed(buf, sem, NP // 2)

    weave = [onehot(iota((2 * NP, NP), 0) == 2 * iota((2 * NP, NP), 1) + f) for f in range(2)]
    part = [onehot(iota((NP, 2 * NP), 1) == 2 * iota((NP, 2 * NP), 0) + f) for f in range(2)]

    def interleave(rows):
        both = dot(weave[0], rows[:, :HALF]) + dot(weave[1], rows[:, HALF:])
        return both.astype(BF).reshape(NP, 2, HALF)

    def separate(rows):
        flat = rows.reshape(2 * NP, HALF)
        return dot(part[0], flat).astype(BF), dot(part[1], flat).astype(BF)

    loads[0].wait()
    loads[1].wait()
    embedded = dot(x_ref[...], emb_ref[...]).astype(BF)
    e_ref[...] = embedded
    s1[...] = interleave(embedded)
    pl.semaphore_wait(barrier, NP + 1)
    scatter_half(s1, h_ref.at[me], p1.at[0], p1.at[2], 0)
    if not THROTTLE1:
        scatter_half(s1, h_ref.at[me], p1.at[1], p1.at[2], 1)
    h_ref[me] = s1[me]
    loads[2].wait()
    wo_copy = remote(wo_ref, wox, wo_sem.at[0], wo_sem.at[1], to_core)
    wo_copy.start()
    if THROTTLE1:
        half_left(s1, p1.at[0], 0)
        scatter_half(s1, h_ref.at[me], p1.at[1], p1.at[2], 1)

    pair_col = dot(
        onehot(iota((2 * NP, NP), 0) // 2 == iota((2 * NP, NP), 1)),
        pairs_ref[...].astype(BF),
        ((1,), (1,)),
    )
    slot_rows = onehot(iota((2 * NP, NP), 0) // 2 == slot_ref[...])
    same = (iota((2 * NP, 2 * NP), 0) - iota((2 * NP, 2 * NP), 1)) % 2 == 0
    pick, spread = [], []
    for b in range(2):
        image = onehot(iota((2 * NP, NP), 1) == pair_col[:, b : b + 1].astype(jnp.int32))
        pick.append(jnp.where(same, dot(image, slot_rows, ((1,), (1,))), 0.0).astype(BF))
        spread.append(jnp.where(same, dot(slot_rows, image, ((1,), (1,))), 0.0).astype(BF))
    uses = jnp.sum(spread[0].astype(F32) + spread[1].astype(F32), axis=1, keepdims=True)

    loads[3].wait()
    for block in range(DD // NP):
        rows = slice(block * NP, (block + 1) * NP)
        wk[rows, :], wv[rows, :] = separate(wkv_ref[rows])
    for load in loads[4:]:
        load.wait()

    landed(h_ref, p1.at[2])
    held = h_ref[...].reshape(2 * NP, HALF)
    for b in range(2):
        s2[b] = dot(pick[b], held).astype(BF).reshape(NP, 2, HALF)
        t_ref[b, me] = s2[b, me]
        for part_no, (first, last) in enumerate(((1, 65), (65, NP))):
            if b and THROTTLE2:
                landed(s2.at[0], p2.at[0, part_no], last - first)
            scatter(s2.at[b], t_ref.at[b, me], p2.at[b, part_no], p2.at[b, 2], first, last)

    def normalize(rows, gain):
        rows = rows.astype(F32)
        centered = rows - jnp.mean(rows, axis=-1, keepdims=True)
        variance = jnp.mean(centered * centered, axis=-1, keepdims=True)
        return (centered * lax.rsqrt(variance + 1e-06) * gain).astype(BF)

    low16 = iota((NP, 128), 1) % 32 < 16

    def rotate(rows, cosine, sine, scale):
        parts = []
        for block in range(HALF // 128):
            u = rows[:, block * 128 : (block + 1) * 128]
            swapped = jnp.where(low16, pltpu.roll(u, 112, 1), pltpu.roll(u, 16, 1))
            parts.append((u * cosine + swapped * sine).astype(BF) * scale)
        return jnp.concatenate(parts, axis=1)

    def image_step(b, carry):
        landed(t_ref.at[b], p2.at[b, 2])
        f_ref[b, mine, :, :HALF], f_ref[b, mine, :, HALF:] = separate(t_ref[b])
        for piece in range(2):
            block = f_ref.at[b, mine, pl.ds(piece * (NP // 2), NP // 2)]
            remote(block, block, ysem.at[b, piece, 0], ysem.at[b, piece, 1], to_view).start()
        block = f_ref.at[b, mine]
        remote(block, block, csem.at[b, 0], csem.at[b, 1], to_core).start()
        there = (1 - view) * 2 + core

        def quarter_step(k, carry):
            quarter = 2 * lax.rem(view + k // 2, 2) + lax.rem(core + k, 2)

            @pl.when(k == 1)
            def _():
                arrive(f_ref.at[b, mine], csem.at[b, 1])

            @pl.when(k == 2)
            def _():
                for piece in range(2):
                    block = f_ref.at[b, there, pl.ds(piece * (NP // 2), NP // 2)]
                    arrive(block, ysem.at[b, piece, 1])
                    remote(
                        block, block, fsem.at[b, piece, 0], fsem.at[b, piece, 1], to_core
                    ).start()

            @pl.when(k == 3)
            def _():
                for piece in range(2):
                    block = f_ref.at[b, there, pl.ds(piece * (NP // 2), NP // 2)]
                    arrive(block, fsem.at[b, piece, 1])

            tokens = f_ref[b, quarter]
            rows = pl.ds(pl.multiple_of(quarter * NP, NP), NP)
            cosine, sine = cos_ref[rows, :], sin_ref[rows, :]

            @pl.when(view == b)
            def _():
                query_in = normalize(tokens, gain_ref[0:1, :])
                qkv[0, rows, :] = rotate(dot(query_in, wq_ref[...]), cosine, sine, BF(HD**-0.5))

            @pl.when(view != b)
            def _():
                key_in = normalize(tokens, gain_ref[1:2, :])
                qkv[1, rows, :] = rotate(dot(key_in, wk[...]), cosine, sine, BF(1.0))
                qkv[2, rows, :] = dot(key_in, wv[...]).astype(BF)

            return carry

        return lax.fori_loop(0, 4, quarter_step, carry)

    lax.fori_loop(0, 2, image_step, 0)
    wo_copy.wait_recv()

    left_q = iota((2 * NP, 128), 1) < HD
    left_k = iota((TOK, 128), 1) < HD
    one = jnp.ones((), BF)
    zero = jnp.zeros((), BF)

    def attend(step, block):
        half = 1 - view if step == 0 else view
        rows = pl.ds(pl.multiple_of(half * 2 * NP, 2 * NP), 2 * NP)
        columns = slice(block * 128, (block + 1) * 128)
        queries = qkv[0, rows, columns]
        keys = qkv[1, :, columns]
        values = qkv[2, :, columns]
        results = []
        for side in range(2):
            own_q = left_q if side == 0 else jnp.logical_not(left_q)
            own_k = left_k if side == 0 else jnp.logical_not(left_k)
            scores = dot(jnp.where(own_q, queries, zero), keys, ((1,), (1,)))
            expo = jnp.exp(scores - jnp.max(scores, axis=-1, keepdims=True)).astype(BF)
            results.append(dot(expo, jnp.where(own_k, values, one)))
        top = jnp.where(left_q, results[0], results[1])
        total = pltpu.roll(jnp.where(left_q, results[1], results[0]), HD, 1)
        attended = (top / total).astype(BF)
        att[step, 0, :, columns] = attended[:NP]
        att[step, 1, :, columns] = attended[NP:]

    def swap_cores(step):
        remote(
            att.at[step, 1 - core], attx.at[step], asem.at[step, 0], asem.at[step, 1], to_core
        ).start()

    def finish(step):
        arrive(attx.at[step], asem.at[step, 1])
        crossed = dot(att[step, core], wo_ref[...], ((1,), (1,)))
        crossed = (crossed + dot(attx[step], wox[...], ((1,), (1,)))).astype(BF)
        s3[step] = interleave(crossed)

    def send_results(step, parity):
        scatter_half(
            s3.at[step], r_ref.at[view, me], p3.at[step, parity], p3.at[step, 2], parity,
            to_view if step == 0 else None,
        )

    for block in range(3):
        attend(0, block)
    swap_cores(0)
    attend(1, 0)
    finish(0)
    send_results(0, 0)
    attend(1, 1)
    attend(1, 2)
    swap_cores(1)
    finish(1)
    send_results(1, 0)
    r_ref[view, me] = s3[1, me]
    if THROTTLE3:
        landed(s3.at[0], p3.at[0, 0], NP // 2)
    send_results(0, 1)
    if THROTTLE3:
        half_left(s3.at[1], p3.at[1, 0], 0)
    send_results(1, 1)

    arrive(r_ref.at[0], p3.at[0, 2])
    landed(r_ref.at[0], p3.at[1, 2])
    total = dot(spread[0], r_ref[0].reshape(2 * NP, HALF))
    total = total + dot(spread[1], r_ref[1].reshape(2 * NP, HALF))
    s4[...] = (total / uses).astype(BF).reshape(NP, 2, HALF)
    scatter(s4, z_ref.at[me], p4.at[0], p4.at[1])
    z_ref[me] = s4[me]
    landed(z_ref, p4.at[1])
    avg_ref[:, :HALF], avg_ref[:, HALF:] = separate(z_ref[...])

    if not THROTTLE1:
        half_left(s1, p1.at[0], 0)
    half_left(s1, p1.at[1], 1)
    wo_copy.wait_send()
    for b in range(2):
        if b or not THROTTLE2:
            landed(s2.at[b], p2.at[b, 0], 64)
            landed(s2.at[b], p2.at[b, 1], 63)
        arrive(f_ref.at[b, mine], csem.at[b, 0])
        for piece in range(2):
            block = f_ref.at[b, mine, pl.ds(piece * (NP // 2), NP // 2)]
            arrive(block, ysem.at[b, piece, 0])
            arrive(block, fsem.at[b, piece, 0])
        arrive(attx.at[b], asem.at[b, 0])
    if not THROTTLE3:
        landed(s3.at[0], p3.at[0, 0], NP // 2)
        half_left(s3.at[1], p3.at[1, 0], 0)
    landed(s3.at[0], p3.at[0, 1], NP // 2)
    half_left(s3.at[1], p3.at[1, 1], 1)
    landed(s4, p4.at[0])


def body(enc_tokens, pairs, image_slot, embed_weight, norm_gains, cross_q, cross_kv, cross_out):
    cosine, sine = rope_tables()
    vmem = pl.BlockSpec(memory_space=pltpu.VMEM)
    far = pl.BlockSpec(memory_space=pl.ANY)
    message = (NP, 2, HALF)
    sems = pltpu.SemaphoreType.DMA
    quarter = jax.ShapeDtypeStruct((NP, DD), BF)
    embedded, average = pl.pallas_call(
        kernel,
        out_shape=(quarter, quarter),
        in_specs=[far, vmem, vmem, far, vmem, far, far, far, far, far],
        out_specs=(vmem, vmem),
        scratch_shapes=[
            pltpu.VMEM((NP, 1024), BF),
            pltpu.VMEM((1024, DD), BF),
            pltpu.VMEM((DD, HALF), BF),
            pltpu.VMEM((DD, 2, HALF), BF),
            pltpu.VMEM((DD, HALF), BF),
            pltpu.VMEM((TOK, 128), F32),
            pltpu.VMEM((TOK, 128), F32),
            pltpu.VMEM(message, BF),
            pltpu.VMEM(message, BF),
            pltpu.VMEM((2,) + message, BF),
            pltpu.VMEM((2,) + message, BF),
            pltpu.VMEM((2, 4, NP, DD), BF),
            pltpu.VMEM((DD, HALF), BF),
            pltpu.VMEM((DD, HALF), BF),
            pltpu.VMEM((DD, HALF), BF),
            pltpu.VMEM((3, TOK, HALF), BF),
            pltpu.VMEM((2, 2, NP, HALF), BF),
            pltpu.VMEM((2, NP, HALF), BF),
            pltpu.VMEM((2,) + message, BF),
            pltpu.VMEM((2,) + message, BF),
            pltpu.VMEM(message, BF),
            pltpu.VMEM(message, BF),
            sems((7,)),
            sems((2,)),
            sems((3,)),
            sems((2, 3)),
            sems((2, 2, 2)),
            sems((2, 2)),
            sems((2, 2, 2)),
            sems((2, 2)),
            sems((2, 3)),
            sems((2,)),
        ],
        compiler_params=pltpu.CompilerParams(
            collective_id=0, has_side_effects=True, vmem_limit_bytes=56 << 20
        ),
        name="cross_block",
    )(
        enc_tokens[0],
        pairs.T,
        image_slot.reshape(1, NP),
        embed_weight,
        norm_gains[0],
        cross_q[0],
        cross_kv[0],
        cross_out[0],
        cosine,
        sine,
    )
    return (embedded.astype(F32) + average.astype(F32)).astype(BF)[None]


def solution(mesh):
    placed = (
        P("pair", ("view", "head"), None),
        P(),
        P(),
        P(),
        P("view", None, None),
        P("view", None, "head"),
        P("view", None, None, "head"),
        P("view", None, "head"),
    )
    return jax.shard_map(
        body,
        mesh=mesh,
        in_specs=placed,
        out_specs=P("pair", ("view", "head"), None),
        check_vma=False,
    )
```

```python
import jax
import jax.numpy as jnp
import numpy as np
from jax import lax
from jax.experimental import pallas as pl
from jax.experimental.pallas import tpu as pltpu
from jax.sharding import PartitionSpec as P

HD = 64
GRIDW = 32
TOK = 512
DD = 768
HALF = 384
NP = 128
BF = jnp.bfloat16
F32 = jnp.float32
MESH = pl.DeviceIdType.MESH
GROUPS = 4
GROUP = NP // GROUPS
CLASSES = 4


def rope_tables():
    lane = np.arange(128)
    token = np.arange(TOK)
    place = np.where(
        ((lane % HD) // 32)[None, :] == 0, (token // GRIDW)[:, None], (token % GRIDW)[:, None]
    ).astype(np.float64)
    frequency = 100.0 ** (-2.0 * (lane % 16) / 32.0)
    angle = place * frequency[None, :]
    sign = np.where((lane % 32) < 16, -1.0, 1.0)
    return np.cos(angle).astype(np.float32), (np.sin(angle) * sign[None, :]).astype(np.float32)


def iota(shape, dim):
    return lax.broadcasted_iota(jnp.int32, shape, dim)


def onehot(mask):
    return jnp.where(mask, 1.0, 0.0).astype(BF)


def dot(a, b, dims=((1,), (0,))):
    return lax.dot_general(a, b, (dims, ((), ())), preferred_element_type=F32)


def kernel(
    x_hbm, pairs_ref, slot_ref, emb_hbm, gain_ref, wq_hbm, wkv_hbm, wo_hbm, cos_hbm, sin_hbm,
    e_ref, avg_ref,
    x_ref, emb_ref, wq_ref, wkv_ref, wo_ref, cos_ref, sin_ref,
    s1, h_ref, s2, t_ref, wk, wv, wox, qkv, att, attx, s3, r_ref, s4, z_ref,
    in_sem, wo_sem, p1, p2_sent, p2_got, y_sent, y_got, c_sem, f_sem, asem, p3, p4,
):
    me = lax.axis_index("pair")
    view = lax.axis_index("view")
    core = lax.axis_index("head")
    to_core = {"head": 1 - core}
    to_view = {"view": 1 - view}

    def remote(src, dst, sent, got, where):
        return pltpu.make_async_remote_copy(
            src, dst, sent, got, device_id=where, device_id_type=MESH
        )

    def arrive(buf, sem):
        pltpu.make_async_copy(buf, buf, sem).wait()

    def landed(buf, sem, count=NP - 1):
        arrive(buf.at[pl.ds(0, count)], sem)

    loads = [
        pltpu.make_async_copy(src, dst, in_sem.at[i])
        for i, (src, dst) in enumerate(
            (
                (x_hbm, x_ref),
                (emb_hbm, emb_ref),
                (wo_hbm, wo_ref),
                (wkv_hbm, wkv_ref),
                (wq_hbm, wq_ref),
                (cos_hbm, cos_ref),
                (sin_hbm, sin_ref),
            )
        )
    ]
    for load in loads:
        load.start()

    barrier = pltpu.get_barrier_semaphore()

    def greet(k, carry):
        pl.semaphore_signal(
            barrier, inc=1, device_id={"pair": lax.rem(me + k, NP)}, device_id_type=MESH
        )
        return carry

    lax.fori_loop(1, NP, greet, 0)
    pl.semaphore_signal(barrier, inc=1, device_id=to_core, device_id_type=MESH)
    pl.semaphore_signal(barrier, inc=1, device_id=to_view, device_id_type=MESH)

    def scatter(src, dst, sent, got, first=1, last=NP, relative=False):
        def send(k, carry):
            peer = lax.rem(me + k, NP)
            place = k if relative else me
            remote(src.at[peer], dst.at[place], sent, got, {"pair": peer}).start()
            return carry

        lax.fori_loop(first, last, send, 0)

    def scatter_class(step, one):
        stride = NP // CLASSES

        def send(i, carry):
            peer = CLASSES * lax.rem(me // CLASSES + i, stride) + one
            target = {"pair": peer, "view": 1 - view if step == 0 else view}
            copy = remote(
                s3.at[step, peer], r_ref.at[view, me], p3.at[step, 0], p3.at[step, 1], target
            )
            if step == 0:
                copy.start()
            else:
                pl.when(peer != me)(copy.start)
            return carry

        lax.fori_loop(0, stride, send, 0)

    weave = [onehot(iota((2 * NP, NP), 0) == 2 * iota((2 * NP, NP), 1) + f) for f in range(2)]
    column, row = iota((NP, 2 * NP), 1), iota((NP, 2 * NP), 0)
    part = [onehot(column == 2 * row + f) for f in range(2)]
    turned = [onehot(column == 2 * lax.rem(me - row + NP, NP) + f) for f in range(2)]

    def interleave(rows):
        both = dot(weave[0], rows[:, :HALF]) + dot(weave[1], rows[:, HALF:])
        return both.astype(BF).reshape(NP, 2, HALF)

    def separate(rows, order):
        flat = rows.reshape(2 * NP, HALF)
        return dot(order[0], flat).astype(BF), dot(order[1], flat).astype(BF)

    loads[0].wait()
    loads[1].wait()
    embedded = dot(x_ref[...], emb_ref[...]).astype(BF)
    e_ref[...] = embedded
    s1[...] = interleave(embedded)
    pl.semaphore_wait(barrier, NP + 1)
    scatter(s1, h_ref, p1.at[0], p1.at[1])
    h_ref[me] = s1[me]
    loads[2].wait()
    wo_copy = remote(wo_ref, wox, wo_sem.at[0], wo_sem.at[1], to_core)
    wo_copy.start()

    pair_col = dot(
        onehot(iota((2 * NP, NP), 0) // 2 == iota((2 * NP, NP), 1)),
        pairs_ref[...].astype(BF),
        ((1,), (1,)),
    )
    slot_rows = onehot(iota((2 * NP, NP), 0) // 2 == slot_ref[...])
    same = (iota((2 * NP, 2 * NP), 0) - iota((2 * NP, 2 * NP), 1)) % 2 == 0
    pick, spread = [], []
    for b in range(2):
        image = onehot(iota((2 * NP, NP), 1) == pair_col[:, b : b + 1].astype(jnp.int32))
        pick.append(jnp.where(same, dot(image, slot_rows, ((1,), (1,))), 0.0).astype(BF))
        spread.append(jnp.where(same, dot(slot_rows, image, ((1,), (1,))), 0.0).astype(BF))
    uses = jnp.sum(spread[0].astype(F32) + spread[1].astype(F32), axis=1, keepdims=True)

    loads[3].wait()
    for block in range(DD // NP):
        rows = slice(block * NP, (block + 1) * NP)
        wk[rows, :], wv[rows, :] = separate(wkv_ref[rows], part)
    for load in loads[4:]:
        load.wait()

    landed(h_ref, p1.at[1])
    held = h_ref[...].reshape(2 * NP, HALF)
    for b in range(2):
        s2[b] = dot(pick[b], held).astype(BF).reshape(NP, 2, HALF)
        for g in range(GROUPS):
            scatter(
                s2.at[b], t_ref.at[b, 0], p2_sent.at[b], p2_got.at[b, g],
                max(g * GROUP, 1), (g + 1) * GROUP, relative=True,
            )
        t_ref[b, 0, 0] = s2[b, me]

    def across(n):
        b, g = divmod(n, GROUPS)
        place = pl.ds(g * GROUP, GROUP)
        new = pl.ds(max(g * GROUP, 1), GROUP if g else GROUP - 1)
        arrive(t_ref.at[b, 0, new], p2_got.at[b, g])
        block = t_ref.at[b, 0, place]
        remote(block, t_ref.at[b, 2, place], y_sent.at[b], y_got.at[b, g], to_view).start()
        remote(block, t_ref.at[b, 1, place], c_sem.at[b, 0], c_sem.at[b, 1], to_core).start()

    def onward(n):
        b, g = divmod(n, GROUPS)
        place = pl.ds(g * GROUP, GROUP)
        block = t_ref.at[b, 2, place]
        arrive(block, y_got.at[b, g])
        remote(block, t_ref.at[b, 3, place], f_sem.at[b, 0], f_sem.at[b, 1], to_core).start()

    for n in range(2 * GROUPS):
        across(n)
        if n >= 2:
            onward(n - 2)

    def normalize(rows, gain):
        rows = rows.astype(F32)
        centered = rows - jnp.mean(rows, axis=-1, keepdims=True)
        variance = jnp.mean(centered * centered, axis=-1, keepdims=True)
        return (centered * lax.rsqrt(variance + 1e-06) * gain).astype(BF)

    low16 = iota((NP, 128), 1) % 32 < 16

    def rotate(rows, cosine, sine, scale):
        parts = []
        for block in range(HALF // 128):
            u = rows[:, block * 128 : (block + 1) * 128]
            swapped = jnp.where(low16, pltpu.roll(u, 112, 1), pltpu.roll(u, 16, 1))
            parts.append((u * cosine + swapped * sine).astype(BF) * scale)
        return jnp.concatenate(parts, axis=1)

    def project(n, carry):
        b, kind = n // 4, n % 4
        quarter = 2 * lax.rem(view + kind // 2, 2) + lax.rem(core + kind, 2)

        @pl.when(n == 1)
        def _():
            onward(2 * GROUPS - 2)

        @pl.when(n == 4)
        def _():
            onward(2 * GROUPS - 1)

        @pl.when(kind == 1)
        def _():
            arrive(t_ref.at[b, 1], c_sem.at[b, 1])

        @pl.when(kind == 3)
        def _():
            arrive(t_ref.at[b, 3], f_sem.at[b, 1])

        tokens = jnp.concatenate(separate(t_ref[b, kind], turned), axis=1)
        rows = pl.ds(pl.multiple_of(quarter * NP, NP), NP)
        cosine, sine = cos_ref[rows, :], sin_ref[rows, :]

        @pl.when(view == b)
        def _():
            query_in = normalize(tokens, gain_ref[0:1, :])
            qkv[0, rows, :] = rotate(dot(query_in, wq_ref[...]), cosine, sine, BF(HD**-0.5))

        @pl.when(view != b)
        def _():
            key_in = normalize(tokens, gain_ref[1:2, :])
            qkv[1, rows, :] = rotate(dot(key_in, wk[...]), cosine, sine, BF(1.0))
            qkv[2, rows, :] = dot(key_in, wv[...]).astype(BF)

        return carry

    lax.fori_loop(0, 8, project, 0)
    wo_copy.wait_recv()

    left_q = iota((2 * NP, 128), 1) < HD
    left_k = iota((TOK, 128), 1) < HD
    one = jnp.ones((), BF)
    zero = jnp.zeros((), BF)

    def attend(step, block):
        half = 1 - view if step == 0 else view
        rows = pl.ds(pl.multiple_of(half * 2 * NP, 2 * NP), 2 * NP)
        columns = slice(block * 128, (block + 1) * 128)
        queries = qkv[0, rows, columns]
        keys = qkv[1, :, columns]
        values = qkv[2, :, columns]
        scores = []
        for side in range(2):
            own_q = left_q if side == 0 else jnp.logical_not(left_q)
            scores.append(dot(jnp.where(own_q, queries, zero), keys, ((1,), (1,))))
        expos = [
            jnp.exp(one_side - jnp.max(one_side, axis=-1, keepdims=True)).astype(BF)
            for one_side in scores
        ]
        results = [
            dot(expos[0], jnp.where(left_k, values, one)),
            dot(expos[1], jnp.where(left_k, one, values)),
        ]
        top = jnp.where(left_q, results[0], results[1])
        total = pltpu.roll(jnp.where(left_q, results[1], results[0]), HD, 1)
        attended = (top / total).astype(BF)
        att[step, 0, :, columns] = attended[:NP]
        att[step, 1, :, columns] = attended[NP:]

    def swap_cores(step):
        remote(
            att.at[step, 1 - core], attx.at[step], asem.at[step, 0], asem.at[step, 1], to_core
        ).start()

    def finish(step):
        arrive(attx.at[step], asem.at[step, 1])
        crossed = dot(att[step, core], wo_ref[...], ((1,), (1,)))
        crossed = (crossed + dot(attx[step], wox[...], ((1,), (1,)))).astype(BF)
        s3[step] = interleave(crossed)

    for block in range(3):
        attend(0, block)
    swap_cores(0)
    attend(1, 0)
    finish(0)
    for one in range(CLASSES // 2):
        scatter_class(0, one)
    attend(1, 1)
    attend(1, 2)
    swap_cores(1)
    finish(1)
    for one in range(CLASSES):
        if one >= CLASSES // 2:
            scatter_class(0, one)
        scatter_class(1, one)
    r_ref[view, me] = s3[1, me]

    arrive(r_ref.at[0], p3.at[0, 1])
    landed(r_ref.at[0], p3.at[1, 1])
    total = dot(spread[0], r_ref[0].reshape(2 * NP, HALF))
    total = total + dot(spread[1], r_ref[1].reshape(2 * NP, HALF))
    s4[...] = (total / uses).astype(BF).reshape(NP, 2, HALF)
    scatter(s4, z_ref, p4.at[0], p4.at[1])
    z_ref[me] = s4[me]
    landed(z_ref, p4.at[1])
    avg_ref[:, :HALF], avg_ref[:, HALF:] = separate(z_ref[...], part)

    landed(s1, p1.at[0])
    wo_copy.wait_send()
    for b in range(2):
        landed(s2.at[b], p2_sent.at[b])
        arrive(t_ref.at[b, 0], y_sent.at[b])
        arrive(t_ref.at[b, 0], c_sem.at[b, 0])
        arrive(t_ref.at[b, 2], f_sem.at[b, 0])
        arrive(attx.at[b], asem.at[b, 0])
    arrive(s3.at[0], p3.at[0, 0])
    landed(s3.at[1], p3.at[1, 0])
    landed(s4, p4.at[0])


def body(enc_tokens, pairs, image_slot, embed_weight, norm_gains, cross_q, cross_kv, cross_out):
    cosine, sine = rope_tables()
    vmem = pl.BlockSpec(memory_space=pltpu.VMEM)
    far = pl.BlockSpec(memory_space=pl.ANY)
    message = (NP, 2, HALF)
    sems = pltpu.SemaphoreType.DMA
    quarter = jax.ShapeDtypeStruct((NP, DD), BF)
    embedded, average = pl.pallas_call(
        kernel,
        out_shape=(quarter, quarter),
        in_specs=[far, vmem, vmem, far, vmem, far, far, far, far, far],
        out_specs=(vmem, vmem),
        scratch_shapes=[
            pltpu.VMEM((NP, 1024), BF),
            pltpu.VMEM((1024, DD), BF),
            pltpu.VMEM((DD, HALF), BF),
            pltpu.VMEM((DD, 2, HALF), BF),
            pltpu.VMEM((DD, HALF), BF),
            pltpu.VMEM((TOK, 128), F32),
            pltpu.VMEM((TOK, 128), F32),
            pltpu.VMEM(message, BF),
            pltpu.VMEM(message, BF),
            pltpu.VMEM((2,) + message, BF),
            pltpu.VMEM((2, 4) + message, BF),
            pltpu.VMEM((DD, HALF), BF),
            pltpu.VMEM((DD, HALF), BF),
            pltpu.VMEM((DD, HALF), BF),
            pltpu.VMEM((3, TOK, HALF), BF),
            pltpu.VMEM((2, 2, NP, HALF), BF),
            pltpu.VMEM((2, NP, HALF), BF),
            pltpu.VMEM((2,) + message, BF),
            pltpu.VMEM((2,) + message, BF),
            pltpu.VMEM(message, BF),
            pltpu.VMEM(message, BF),
            sems((7,)),
            sems((2,)),
            sems((2,)),
            sems((2,)),
            sems((2, GROUPS)),
            sems((2,)),
            sems((2, GROUPS)),
            sems((2, 2)),
            sems((2, 2)),
            sems((2, 2)),
            sems((2, 2)),
            sems((2,)),
        ],
        compiler_params=pltpu.CompilerParams(
            collective_id=0, has_side_effects=True, vmem_limit_bytes=56 << 20
        ),
        name="cross_block",
    )(
        enc_tokens[0],
        pairs.T,
        image_slot.reshape(1, NP),
        embed_weight,
        norm_gains[0],
        cross_q[0],
        cross_kv[0],
        cross_out[0],
        cosine,
        sine,
    )
    return (embedded.astype(F32) + average.astype(F32)).astype(BF)[None]


def solution(mesh):
    placed = (
        P("pair", ("view", "head"), None),
        P(),
        P(),
        P(),
        P("view", None, None),
        P("view", None, "head"),
        P("view", None, None, "head"),
        P("view", None, "head"),
    )
    return jax.shard_map(
        body,
        mesh=mesh,
        in_specs=placed,
        out_specs=P("pair", ("view", "head"), None),
        check_vma=False,
    )
```

```python
import jax
import jax.numpy as jnp
import numpy as np
from jax import lax
from jax.experimental import pallas as pl
from jax.experimental.pallas import tpu as pltpu
from jax.sharding import PartitionSpec as P

HD = 64
GRIDW = 32
TOK = 512
DD = 768
HALF = 384
NP = 128
BF = jnp.bfloat16
F32 = jnp.float32
MESH = pl.DeviceIdType.MESH
GROUPS = 4
GROUP = NP // GROUPS
CLASSES = 4


def rope_tables():
    lane = np.arange(128)
    token = np.arange(TOK)
    place = np.where(
        ((lane % HD) // 32)[None, :] == 0, (token // GRIDW)[:, None], (token % GRIDW)[:, None]
    ).astype(np.float64)
    frequency = 100.0 ** (-2.0 * (lane % 16) / 32.0)
    angle = place * frequency[None, :]
    sign = np.where((lane % 32) < 16, -1.0, 1.0)
    return np.cos(angle).astype(np.float32), (np.sin(angle) * sign[None, :]).astype(np.float32)


def iota(shape, dim):
    return lax.broadcasted_iota(jnp.int32, shape, dim)


def onehot(mask):
    return jnp.where(mask, 1.0, 0.0).astype(BF)


def dot(a, b, dims=((1,), (0,))):
    return lax.dot_general(a, b, (dims, ((), ())), preferred_element_type=F32)


def kernel(
    x_hbm, pairs_ref, slot_ref, emb_hbm, gain_ref, wq_hbm, wkv_hbm, wo_hbm, cos_hbm, sin_hbm,
    e_ref, avg_ref,
    x_ref, emb_ref, wq_ref, wkv_ref, wo_ref, cos_ref, sin_ref,
    s1, h_ref, s2, t_ref, wk, wv, wox, qkv, att, attx, s3, r_ref, s4, z_ref,
    in_sem, wo_sem, p1, p2_sent, p2_got, y_sent, y_got, c_sem, f_sem, asem, p3, p4,
):
    me = lax.axis_index("pair")
    view = lax.axis_index("view")
    core = lax.axis_index("head")
    to_core = {"head": 1 - core}
    to_view = {"view": 1 - view}

    def remote(src, dst, sent, got, where):
        return pltpu.make_async_remote_copy(
            src, dst, sent, got, device_id=where, device_id_type=MESH
        )

    def arrive(buf, sem):
        pltpu.make_async_copy(buf, buf, sem).wait()

    def landed(buf, sem, count=NP - 1):
        arrive(buf.at[pl.ds(0, count)], sem)

    loads = [
        pltpu.make_async_copy(src, dst, in_sem.at[i])
        for i, (src, dst) in enumerate(
            (
                (x_hbm, x_ref),
                (emb_hbm, emb_ref),
                (wo_hbm, wo_ref),
                (wkv_hbm, wkv_ref),
                (wq_hbm, wq_ref),
                (cos_hbm, cos_ref),
                (sin_hbm, sin_ref),
            )
        )
    ]
    for load in loads:
        load.start()

    barrier = pltpu.get_barrier_semaphore()

    def greet(k, carry):
        pl.semaphore_signal(
            barrier, inc=1, device_id={"pair": lax.rem(me + k, NP)}, device_id_type=MESH
        )
        return carry

    lax.fori_loop(1, NP, greet, 0)
    pl.semaphore_signal(barrier, inc=1, device_id=to_core, device_id_type=MESH)
    pl.semaphore_signal(barrier, inc=1, device_id=to_view, device_id_type=MESH)

    def scatter(src, dst, sent, got, first=1, last=NP, relative=False):
        def send(k, carry):
            peer = lax.rem(me + k, NP)
            place = k if relative else me
            remote(src.at[peer], dst.at[place], sent, got, {"pair": peer}).start()
            return carry

        lax.fori_loop(first, last, send, 0)

    def scatter_class(step, one):
        stride = NP // CLASSES

        def send(i, carry):
            peer = CLASSES * lax.rem(me // CLASSES + i, stride) + one
            target = {"pair": peer, "view": 1 - view if step == 0 else view}
            copy = remote(
                s3.at[step, peer], r_ref.at[view, me], p3.at[step, 0], p3.at[step, 1], target
            )
            if step == 0:
                copy.start()
            else:
                pl.when(peer != me)(copy.start)
            return carry

        lax.fori_loop(0, stride, send, 0)

    weave = [onehot(iota((2 * NP, NP), 0) == 2 * iota((2 * NP, NP), 1) + f) for f in range(2)]
    column, row = iota((NP, 2 * NP), 1), iota((NP, 2 * NP), 0)
    part = [onehot(column == 2 * row + f) for f in range(2)]
    turned = [onehot(column == 2 * lax.rem(me - row + NP, NP) + f) for f in range(2)]

    def interleave(rows):
        both = dot(weave[0], rows[:, :HALF]) + dot(weave[1], rows[:, HALF:])
        return both.astype(BF).reshape(NP, 2, HALF)

    def separate(rows, order):
        flat = rows.reshape(2 * NP, HALF)
        return dot(order[0], flat).astype(BF), dot(order[1], flat).astype(BF)

    loads[0].wait()
    loads[1].wait()
    embedded = dot(x_ref[...], emb_ref[...]).astype(BF)
    e_ref[...] = embedded
    s1[...] = interleave(embedded)
    pl.semaphore_wait(barrier, NP + 1)
    scatter(s1, h_ref, p1.at[0], p1.at[1])
    h_ref[me] = s1[me]
    loads[2].wait()
    wo_copy = remote(wo_ref, wox, wo_sem.at[0], wo_sem.at[1], to_core)
    wo_copy.start()

    pair_col = dot(
        onehot(iota((2 * NP, NP), 0) // 2 == iota((2 * NP, NP), 1)),
        pairs_ref[...].astype(BF),
        ((1,), (1,)),
    )
    slot_rows = onehot(iota((2 * NP, NP), 0) // 2 == slot_ref[...])
    same = (iota((2 * NP, 2 * NP), 0) - iota((2 * NP, 2 * NP), 1)) % 2 == 0
    pick, spread = [], []
    for b in range(2):
        image = onehot(iota((2 * NP, NP), 1) == pair_col[:, b : b + 1].astype(jnp.int32))
        pick.append(jnp.where(same, dot(image, slot_rows, ((1,), (1,))), 0.0).astype(BF))
        spread.append(jnp.where(same, dot(slot_rows, image, ((1,), (1,))), 0.0).astype(BF))
    uses = jnp.sum(spread[0].astype(F32) + spread[1].astype(F32), axis=1, keepdims=True)

    loads[3].wait()
    for block in range(DD // NP):
        rows = slice(block * NP, (block + 1) * NP)
        wk[rows, :], wv[rows, :] = separate(wkv_ref[rows], part)
    for load in loads[4:]:
        load.wait()

    landed(h_ref, p1.at[1])
    held = h_ref[...].reshape(2 * NP, HALF)
    for b in range(2):
        s2[b] = dot(pick[b], held).astype(BF).reshape(NP, 2, HALF)
        for g in range(GROUPS):
            scatter(
                s2.at[b], t_ref.at[b, 0], p2_sent.at[b], p2_got.at[b, g],
                max(g * GROUP, 1), (g + 1) * GROUP, relative=True,
            )
        t_ref[b, 0, 0] = s2[b, me]

    def across(n):
        b, g = divmod(n, GROUPS)
        place = pl.ds(g * GROUP, GROUP)
        new = pl.ds(max(g * GROUP, 1), GROUP if g else GROUP - 1)
        arrive(t_ref.at[b, 0, new], p2_got.at[b, g])
        block = t_ref.at[b, 0, place]
        remote(block, t_ref.at[b, 2, place], y_sent.at[b], y_got.at[b, g], to_view).start()
        remote(block, t_ref.at[b, 1, place], c_sem.at[b, 0], c_sem.at[b, 1], to_core).start()

    def onward(n):
        b, g = divmod(n, GROUPS)
        place = pl.ds(g * GROUP, GROUP)
        block = t_ref.at[b, 2, place]
        arrive(block, y_got.at[b, g])
        remote(block, t_ref.at[b, 3, place], f_sem.at[b, 0], f_sem.at[b, 1], to_core).start()

    def normalize(rows, gain):
        rows = rows.astype(F32)
        centered = rows - jnp.mean(rows, axis=-1, keepdims=True)
        variance = jnp.mean(centered * centered, axis=-1, keepdims=True)
        return (centered * lax.rsqrt(variance + 1e-06) * gain).astype(BF)

    low16 = iota((NP, 128), 1) % 32 < 16

    def rotate(rows, cosine, sine, scale):
        parts = []
        for block in range(HALF // 128):
            u = rows[:, block * 128 : (block + 1) * 128]
            swapped = jnp.where(low16, pltpu.roll(u, 112, 1), pltpu.roll(u, 16, 1))
            parts.append((u * cosine + swapped * sine).astype(BF) * scale)
        return jnp.concatenate(parts, axis=1)

    def project(n, carry):
        b, kind = n // 4, n % 4
        quarter = 2 * lax.rem(view + kind // 2, 2) + lax.rem(core + kind, 2)

        @pl.when(n == 5)
        def _():
            onward(2 * GROUPS - 1)

        @pl.when(kind == 1)
        def _():
            arrive(t_ref.at[b, 1], c_sem.at[b, 1])

        @pl.when(kind == 3)
        def _():
            arrive(t_ref.at[b, 3], f_sem.at[b, 1])

        tokens = jnp.concatenate(separate(t_ref[b, kind], turned), axis=1)
        rows = pl.ds(pl.multiple_of(quarter * NP, NP), NP)
        cosine, sine = cos_ref[rows, :], sin_ref[rows, :]

        @pl.when(view == b)
        def _():
            query_in = normalize(tokens, gain_ref[0:1, :])
            qkv[0, rows, :] = rotate(dot(query_in, wq_ref[...]), cosine, sine, BF(HD**-0.5))

        @pl.when(view != b)
        def _():
            key_in = normalize(tokens, gain_ref[1:2, :])
            qkv[1, rows, :] = rotate(dot(key_in, wk[...]), cosine, sine, BF(1.0))
            qkv[2, rows, :] = dot(key_in, wv[...]).astype(BF)

        return carry

    for n in range(2 * GROUPS):
        across(n)
        if n >= 2:
            onward(n - 2)
        if 0 <= n - GROUPS < 3:
            project(n - GROUPS, 0)
    onward(2 * GROUPS - 2)
    lax.fori_loop(3, 8, project, 0)
    wo_copy.wait_recv()

    left_q = iota((2 * NP, 128), 1) < HD
    left_k = iota((TOK, 128), 1) < HD
    one = jnp.ones((), BF)
    zero = jnp.zeros((), BF)

    def attend(step, block):
        half = 1 - view if step == 0 else view
        rows = pl.ds(pl.multiple_of(half * 2 * NP, 2 * NP), 2 * NP)
        columns = slice(block * 128, (block + 1) * 128)
        queries = qkv[0, rows, columns]
        keys = qkv[1, :, columns]
        values = qkv[2, :, columns]
        scores = []
        for side in range(2):
            own_q = left_q if side == 0 else jnp.logical_not(left_q)
            scores.append(dot(jnp.where(own_q, queries, zero), keys, ((1,), (1,))))
        expos = [
            jnp.exp(one_side - jnp.max(one_side, axis=-1, keepdims=True)).astype(BF)
            for one_side in scores
        ]
        results = [
            dot(expos[0], jnp.where(left_k, values, one)),
            dot(expos[1], jnp.where(left_k, one, values)),
        ]
        top = jnp.where(left_q, results[0], results[1])
        total = pltpu.roll(jnp.where(left_q, results[1], results[0]), HD, 1)
        attended = (top / total).astype(BF)
        att[step, 0, :, columns] = attended[:NP]
        att[step, 1, :, columns] = attended[NP:]

    def swap_cores(step):
        remote(
            att.at[step, 1 - core], attx.at[step], asem.at[step, 0], asem.at[step, 1], to_core
        ).start()

    def finish(step):
        arrive(attx.at[step], asem.at[step, 1])
        crossed = dot(att[step, core], wo_ref[...], ((1,), (1,)))
        crossed = (crossed + dot(attx[step], wox[...], ((1,), (1,)))).astype(BF)
        s3[step] = interleave(crossed)

    for block in range(3):
        attend(0, block)
    swap_cores(0)
    attend(1, 0)
    finish(0)
    for one in range(CLASSES // 2):
        scatter_class(0, one)
    attend(1, 1)
    attend(1, 2)
    swap_cores(1)
    finish(1)
    for one in range(CLASSES):
        if one >= CLASSES // 2:
            scatter_class(0, one)
        scatter_class(1, one)
    r_ref[view, me] = s3[1, me]

    arrive(r_ref.at[0], p3.at[0, 1])
    landed(r_ref.at[0], p3.at[1, 1])
    total = dot(spread[0], r_ref[0].reshape(2 * NP, HALF))
    total = total + dot(spread[1], r_ref[1].reshape(2 * NP, HALF))
    s4[...] = (total / uses).astype(BF).reshape(NP, 2, HALF)
    scatter(s4, z_ref, p4.at[0], p4.at[1])
    z_ref[me] = s4[me]
    landed(z_ref, p4.at[1])
    avg_ref[:, :HALF], avg_ref[:, HALF:] = separate(z_ref[...], part)

    landed(s1, p1.at[0])
    wo_copy.wait_send()
    for b in range(2):
        landed(s2.at[b], p2_sent.at[b])
        arrive(t_ref.at[b, 0], y_sent.at[b])
        arrive(t_ref.at[b, 0], c_sem.at[b, 0])
        arrive(t_ref.at[b, 2], f_sem.at[b, 0])
        arrive(attx.at[b], asem.at[b, 0])
    arrive(s3.at[0], p3.at[0, 0])
    landed(s3.at[1], p3.at[1, 0])
    landed(s4, p4.at[0])


def body(enc_tokens, pairs, image_slot, embed_weight, norm_gains, cross_q, cross_kv, cross_out):
    cosine, sine = rope_tables()
    vmem = pl.BlockSpec(memory_space=pltpu.VMEM)
    far = pl.BlockSpec(memory_space=pl.ANY)
    message = (NP, 2, HALF)
    sems = pltpu.SemaphoreType.DMA
    quarter = jax.ShapeDtypeStruct((NP, DD), BF)
    embedded, average = pl.pallas_call(
        kernel,
        out_shape=(quarter, quarter),
        in_specs=[far, vmem, vmem, far, vmem, far, far, far, far, far],
        out_specs=(vmem, vmem),
        scratch_shapes=[
            pltpu.VMEM((NP, 1024), BF),
            pltpu.VMEM((1024, DD), BF),
            pltpu.VMEM((DD, HALF), BF),
            pltpu.VMEM((DD, 2, HALF), BF),
            pltpu.VMEM((DD, HALF), BF),
            pltpu.VMEM((TOK, 128), F32),
            pltpu.VMEM((TOK, 128), F32),
            pltpu.VMEM(message, BF),
            pltpu.VMEM(message, BF),
            pltpu.VMEM((2,) + message, BF),
            pltpu.VMEM((2, 4) + message, BF),
            pltpu.VMEM((DD, HALF), BF),
            pltpu.VMEM((DD, HALF), BF),
            pltpu.VMEM((DD, HALF), BF),
            pltpu.VMEM((3, TOK, HALF), BF),
            pltpu.VMEM((2, 2, NP, HALF), BF),
            pltpu.VMEM((2, NP, HALF), BF),
            pltpu.VMEM((2,) + message, BF),
            pltpu.VMEM((2,) + message, BF),
            pltpu.VMEM(message, BF),
            pltpu.VMEM(message, BF),
            sems((7,)),
            sems((2,)),
            sems((2,)),
            sems((2,)),
            sems((2, GROUPS)),
            sems((2,)),
            sems((2, GROUPS)),
            sems((2, 2)),
            sems((2, 2)),
            sems((2, 2)),
            sems((2, 2)),
            sems((2,)),
        ],
        compiler_params=pltpu.CompilerParams(
            collective_id=0, has_side_effects=True, vmem_limit_bytes=56 << 20
        ),
        name="cross_block",
    )(
        enc_tokens[0],
        pairs.T,
        image_slot.reshape(1, NP),
        embed_weight,
        norm_gains[0],
        cross_q[0],
        cross_kv[0],
        cross_out[0],
        cosine,
        sine,
    )
    return (embedded.astype(F32) + average.astype(F32)).astype(BF)[None]


def solution(mesh):
    placed = (
        P("pair", ("view", "head"), None),
        P(),
        P(),
        P(),
        P("view", None, None),
        P("view", None, "head"),
        P("view", None, None, "head"),
        P("view", None, "head"),
    )
    return jax.shard_map(
        body,
        mesh=mesh,
        in_specs=placed,
        out_specs=P("pair", ("view", "head"), None),
        check_vma=False,
    )
```
